32 devices in a mesh: groups: 2 (over y), dp: 4 (over x, core), tensor: 4 (over z).
Axes of the slice: x: 2, y: 2, z: 4, core: 2. Of those that a mesh axis runs over, the one named last changes fastest.
Arguments:
- acts: bfloat16 [32768, 4096], P(('groups', 'dp'), 'tensor'), parts along dimension 0, may hold values from -12 to 12
- out_grads: bfloat16 [32768, 14336], P(('groups', 'dp'), 'tensor'), parts along dimension 0, may hold values from -12 to 12
- proj_in: bfloat16 [32, 4096], replicated, may hold values from -0.09375 to 0.09375
- proj_out: bfloat16 [32, 14336], replicated, may hold values from -0.046875 to 0.046875
- query_acts: bfloat16 [4096, 4096], P(('groups', 'tensor'), 'dp'), parts along dimension 0, may hold values from -48 to 48
- query_grads: bfloat16 [4096, 14336], P(('groups', 'tensor'), 'dp'), parts along dimension 0, may hold values from -48 to 48
Outputs:
- scores: float32 [4096, 512], P(('groups', 'dp', 'tensor')), parts along dimension 0
The draws below stay inside these ranges and needn't reach their ends.
There are 2 independent parts, one for each index of `groups`. The reference program is written for one: setup_inputs(seed, part) draws one part's arguments, and reference() takes and returns one part's arrays. A program takes and returns all parts, laid end to end along the dimension named above; an argument that names none is the same for every part. Nothing has to cross between parts.
All inputs are finite; a program needn't handle non-finite values.
Results may differ from the reference program's by a relative error of at most 0.0003.
Values sent between devices are 32-bit elements; how exact they have to be, the bound alone decides.
No kernel may reach another device: no remote copies, remote signals or barrier semaphores. Data moves between devices by JAX's collectives and lax.ppermute only.
A program may use at most 192 MiB of HBM per device.

```python
import jax
import jax.numpy as jnp
from jax import lax

D = 4096
FF = 14336
RANK = 32
SEQ = 8
QLEN = 4
EXAMPLES = 2048
TOKENS = 16384
QTOK = 2048


def sequence_classes(key):
    return jax.random.randint(jax.random.fold_in(key, 11), (EXAMPLES,), 0, 4)


def drawn(key, columns, classes):
    latent_table = jax.random.normal(jax.random.fold_in(key, 1), (4, SEQ, columns), jnp.float32)
    token_class = jnp.repeat(classes, SEQ)
    position = jnp.arange(TOKENS, dtype=jnp.int32) % SEQ
    return latent_table[token_class, position]


def mixture(key, columns, classes):
    latent = drawn(key, columns, classes)
    amplitude = 2.0
    base = jax.random.normal(jax.random.fold_in(key, 2), (TOKENS, columns), jnp.float32)
    return jnp.clip(base + amplitude * latent, -12.0, 12.0).astype(jnp.bfloat16)


def draw_acts(key, part):
    classes = sequence_classes(key)
    key = jax.random.fold_in(key, 3)
    return mixture(key, D, classes)


def draw_out_grads(key, part):
    classes = sequence_classes(key)
    key = jax.random.fold_in(key, 5)
    return mixture(key, FF, classes)


def block_scale(own_key, dims, cuts, low, top_value):
    factor_of, own = 1.0, jax.random.fold_in(own_key, 6)
    for dim, shards_of in cuts:
        steps = jnp.exp(jax.random.uniform(jax.random.fold_in(own, dim), (shards_of,), jnp.float32, low / len(cuts), top_value / len(cuts)))
        factor_of = factor_of * jnp.repeat(steps, dims[dim] // shards_of).reshape([-1 if axis == dim else 1 for axis in range(len(dims))])
    return factor_of


def bell_draw(key, dims, scale, bound, split=(), kind=jnp.bfloat16):
    entries = jax.random.normal(key, dims, jnp.float32) * scale
    if len(split) > 0:
        entries = block_scale(key, dims, split, -0.22, 0.18) * entries
    return jnp.clip(entries, min=-bound, max=bound).astype(kind)


def setup_inputs(seed: int = 0, part: int = 0) -> dict:
    streams_of = jax.random.split(jax.random.key(seed), 7)
    own_keys = jax.random.split(jax.random.fold_in(streams_of[6], part), 7)
    return {
        "acts": draw_acts(jax.random.fold_in(jax.random.fold_in(streams_of[6], part), 71), part),
        "out_grads": draw_out_grads(jax.random.fold_in(jax.random.fold_in(streams_of[6], part), 71), part),
        "proj_in": bell_draw(streams_of[2], (RANK, D), D ** -0.5, 0.09375),
        "proj_out": bell_draw(streams_of[3], (RANK, FF), FF ** -0.5, 0.046875),
        "query_acts": bell_draw(own_keys[4], (QTOK, D), 8.0, 48.0, ((0, 4), (1, 4))),
        "query_grads": bell_draw(own_keys[5], (QTOK, FF), 8.0, 48.0, ((0, 4), (1, 4))),
    }


def project(rows, proj):
    return lax.dot_general(rows.astype(jnp.float32), proj.astype(jnp.float32), (((1,), (1,)), ((), ())), preferred_element_type=jnp.float32)

def example_grads(outs, ins, length):
    count = outs.shape[0] // length
    rank = outs.shape[1]
    outer = jnp.einsum('esa,esb->eab', outs.reshape(count, length, rank), ins.reshape(count, length, rank), precision=lax.Precision.HIGHEST)
    return outer.reshape(count, rank * rank)

def reference(acts, out_grads, proj_in, proj_out, query_acts, query_grads):
    grads = example_grads(project(out_grads, proj_out), project(acts, proj_in), SEQ)
    qgrads = example_grads(project(query_grads, proj_out), project(query_acts, proj_in), QLEN)
    fisher = lax.dot_general(grads, grads, (((0,), (0,)), ((), ())), precision=lax.Precision.HIGHEST)
    size = fisher.shape[0]
    damped = fisher + 0.1 * jnp.trace(fisher) / size * jnp.eye(size, dtype=jnp.float32)
    chol = jnp.linalg.cholesky(damped)
    white_q = lax.linalg.triangular_solve(chol, qgrads.T, left_side=True, lower=True)
    white_g = lax.linalg.triangular_solve(chol, grads.T, left_side=True, lower=True)
    return lax.dot_general(white_g, white_q, (((0,), (0,)), ((), ())), precision=lax.Precision.HIGHEST)
```

```python
import functools

import jax
import jax.numpy as jnp
from jax import lax
from jax.experimental import pallas as pl
from jax.experimental.pallas import tpu as pltpu
from jax.sharding import PartitionSpec as P

SEQ = 8
QLEN = 4
RANK = 32
SIZE = RANK * RANK
LANES = 128
TILE = 128
BLOCKS = SIZE // TILE
VMEM = 56 * 1024 * 1024
F32 = jnp.float32
BF16 = jnp.bfloat16
TN = (((0,), (0,)), ((), ()))
NT = (((1,), (1,)), ((), ()))


def project_kernel(length, steps, ins_ref, outs_ref, pin_ref, pout_ref, o_ref, rows_ref):
    step = pl.program_id(0)
    rows = ins_ref.shape[0]
    value = lax.dot_general(outs_ref[...], pout_ref[...], NT, preferred_element_type=F32)
    value += lax.dot_general(ins_ref[...], pin_ref[...], NT, preferred_element_type=F32)
    rows_ref[pl.ds(pl.multiple_of(lax.rem(step, steps) * rows, rows), rows), :] = value

    @pl.when(lax.rem(step, steps) == steps - 1)
    def _():
        for t in range(length):
            o_ref[0, t * 2 * RANK : (t + 1) * 2 * RANK, :] = rows_ref[pl.ds(t, o_ref.shape[2], stride=length), :].T[: 2 * RANK]


def project(ins, outs, proj_in, proj_out, length, rows):
    tokens = ins.shape[0]
    group = min(LANES, tokens // length)
    rows = min(rows, group * length)
    steps = group * length // rows
    pin = jnp.pad(proj_in, ((RANK, LANES - 2 * RANK), (0, 0)))
    pout = jnp.pad(proj_out, ((0, LANES - RANK), (0, 0)))
    whole = lambda arr: pl.BlockSpec(arr.shape, lambda i: (0, 0))
    return pl.pallas_call(
        functools.partial(project_kernel, length, steps),
        out_shape=jax.ShapeDtypeStruct((tokens // (group * length), length * 2 * RANK, group), F32),
        grid=(tokens // rows,),
        in_specs=[
            pl.BlockSpec((rows, ins.shape[1]), lambda i: (i, 0)),
            pl.BlockSpec((rows, outs.shape[1]), lambda i: (i, 0)),
            whole(pin),
            whole(pout),
        ],
        out_specs=pl.BlockSpec((1, length * 2 * RANK, group), lambda i: (i // steps, 0, 0)),
        scratch_shapes=[pltpu.VMEM((group * length, LANES), F32)],
        compiler_params=pltpu.CompilerParams(vmem_limit_bytes=VMEM),
    )(ins, outs, pin, pout)


def outer_rows(tok, length, a):
    total = None
    for t in range(length):
        base = t * 2 * RANK
        term = tok[base + a : base + a + 1, :] * tok[base + RANK : base + 2 * RANK, :]
        total = term if total is None else total + term
    return total


def split2(x):
    hi = x.astype(BF16)
    return hi, (x - hi.astype(F32)).astype(BF16)


def split3(x):
    hi = x.astype(BF16)
    rest = x - hi.astype(F32)
    mid = rest.astype(BF16)
    return hi, mid, (rest - mid.astype(F32)).astype(BF16)


def gram_kernel(tok_ref, f_ref, x_ref, y_ref):
    @pl.when(pl.program_id(0) == 0)
    def _():
        f_ref[...] = jnp.zeros_like(f_ref)

    count = tok_ref.shape[0]
    width = count * LANES
    for s in range(count):
        for a in range(RANK):
            hi, lo = split2(outer_rows(tok_ref.at[s], SEQ, a))
            row = slice(a * RANK, (a + 1) * RANK)
            for ref, parts in ((x_ref, (hi, hi, lo)), (y_ref, (hi, lo, hi))):
                for q, part in enumerate(parts):
                    ref[row, q * width + s * LANES : q * width + (s + 1) * LANES] = part
    big = 256
    for r in range(SIZE // big):
        rows = slice(r * big, (r + 1) * big)
        f_ref[rows, r * big :] += lax.dot_general(x_ref[rows, :], y_ref[r * big :, :], NT, preferred_element_type=F32)


def gram(tok):
    count = 2 if tok.shape[0] % 2 == 0 else 1
    return pl.pallas_call(
        gram_kernel,
        out_shape=jax.ShapeDtypeStruct((SIZE, SIZE), F32),
        grid=(tok.shape[0] // count,),
        in_specs=[pl.BlockSpec((count,) + tok.shape[1:], lambda i: (i, 0, 0))],
        out_specs=pl.BlockSpec((SIZE, SIZE), lambda i: (0, 0)),
        scratch_shapes=[pltpu.VMEM((SIZE, 3 * count * LANES), BF16)] * 2,
        compiler_params=pltpu.CompilerParams(vmem_limit_bytes=VMEM),
    )(tok)


AHEAD = 2


def lanes_of(x, k):
    return jnp.broadcast_to(x[:, k : k + 1], (8, LANES))


def row_of(x, j):
    return jnp.broadcast_to(x[j : j + 1, :], (8, LANES))


def inverse_factor(groups):
    lane = lax.broadcasted_iota(jnp.int32, (8, LANES), 1)
    sub = lax.broadcasted_iota(jnp.int32, (8, LANES), 0)
    groups = list(groups)
    count = len(groups)
    pivots = [None] * count
    for p in range(count):
        panel = (lane >= 8 * p) & (lane < 8 * p + 8)
        near = range(p, min(p + 1 + AHEAD, count))
        far = range(min(p + 1 + AHEAD, count), count)
        cols = {i: [lanes_of(groups[i], 8 * p + k) for k in range(8)] for i in near}
        for i in near:
            groups[i] = jnp.where(panel, 0.0, groups[i])
        groups[p] = jnp.where(lane == sub + 8 * p, 1.0, groups[p])
        pivot = jnp.zeros((8, LANES), F32)
        scale = jnp.zeros((8, LANES), F32)
        for j in range(8):
            diag = row_of(cols[p][j], j)
            inv = -1.0 / diag
            pivot = jnp.where(sub == j, diag, pivot)
            scale = jnp.where(sub == j, inv, scale)
            row = row_of(groups[p], j)
            tops = [row_of(cols[p][k], j) for k in range(8)]
            for i in near:
                mult = cols[i][j] * inv
                if i == p:
                    mult = jnp.where(sub > j, mult, 0.0)
                for k in range(j + 1, 8):
                    cols[i][k] = cols[i][k] + mult * tops[k]
                groups[i] = groups[i] + mult * row
        pivots[p] = pivot
        if len(far) > 0:
            update = lax.dot_general(
                groups[p] * scale, groups[p], TN, precision=lax.Precision.HIGHEST, preferred_element_type=F32
            )
            for i in far:
                groups[i] = jnp.where(panel, 0.0, groups[i]) + update[8 * i : 8 * i + 8]
    return [
        jnp.where(lane <= sub + 8 * p, groups[p], 0.0) * lax.rsqrt(pivots[p]) for p in range(count)
    ]


def pair_left(parts, axis):
    hi, mid, lo = parts
    return jnp.concatenate([hi, hi, mid, mid, hi, lo], axis=axis)


def pair_right(parts, axis):
    hi, mid, lo = parts
    return jnp.concatenate([hi, mid, hi, mid, lo, hi], axis=axis)


def solve_kernel(f_ref, own_ref, query_ref, o_ref, a_ref, r_ref, x_ref, y_ref):
    for a in range(RANK):
        rows = slice(a * RANK, (a + 1) * RANK)
        r_ref[rows, :LANES] = outer_rows(own_ref, SEQ, a)
        for s in range(query_ref.shape[0]):
            r_ref[rows, (s + 1) * LANES : (s + 2) * LANES] = outer_rows(query_ref.at[s], QLEN, a)
    eye = lax.broadcasted_iota(jnp.int32, (TILE, TILE), 0) == lax.broadcasted_iota(jnp.int32, (TILE, TILE), 1)
    total = jnp.zeros((TILE, TILE), F32)
    for b in range(BLOCKS):
        rows = slice(b * TILE, (b + 1) * TILE)
        total += jnp.where(eye, f_ref[rows, rows], 0.0)
    damping = 0.1 / SIZE * jnp.sum(total)
    for b in range(BLOCKS):
        rows = slice(b * TILE, (b + 1) * TILE)
        rest = slice((b + 1) * TILE, SIZE)
        src = f_ref if b == 0 else a_ref
        block = src[rows, rows] + jnp.where(eye, damping, 0.0)
        inv = jnp.concatenate(inverse_factor([block[8 * p : 8 * p + 8] for p in range(TILE // 8)]), axis=0)
        left = pair_left(split3(inv), 1)
        if b + 1 < BLOCKS:
            w = lax.dot_general(left, pair_right(split3(src[rows, rest]), 0), (((1,), (0,)), ((), ())), preferred_element_type=F32)
            parts = split3(w)
            x_ref[:, rest] = pair_left(parts, 0)
            y_ref[:, rest] = pair_right(parts, 0)
        wr = lax.dot_general(left, pair_right(split3(r_ref[rows, :]), 0), (((1,), (0,)), ((), ())), preferred_element_type=F32)
        r_ref[rows, :] = wr
        y_ref[:, SIZE:] = pair_right(split3(wr), 0)
        for i in range(b + 1, BLOCKS):
            mine = slice(i * TILE, (i + 1) * TILE)
            right = slice(i * TILE, SIZE)
            delta = lax.dot_general(x_ref[:, mine], y_ref[:, i * TILE :], TN, preferred_element_type=F32)
            a_ref[mine, right] = src[mine, right] - delta[:, : SIZE - i * TILE]
            r_ref[mine, :] -= delta[:, SIZE - i * TILE :]
    o_ref[...] = lax.dot_general(
        r_ref[:, :LANES], r_ref[:, LANES:], TN, precision=lax.Precision.HIGHEST, preferred_element_type=F32
    )


def solve(fisher, own, query):
    width = (1 + query.shape[0]) * LANES
    return pl.pallas_call(
        solve_kernel,
        out_shape=jax.ShapeDtypeStruct((LANES, width - LANES), F32),
        in_specs=[pl.BlockSpec(memory_space=pltpu.VMEM)] * 3,
        out_specs=pl.BlockSpec(memory_space=pltpu.VMEM),
        scratch_shapes=[
            pltpu.VMEM((SIZE, SIZE), F32),
            pltpu.VMEM((SIZE, width), F32),
            pltpu.VMEM((6 * TILE, SIZE), BF16),
            pltpu.VMEM((6 * TILE, SIZE + width), BF16),
        ],
        compiler_params=pltpu.CompilerParams(vmem_limit_bytes=VMEM),
    )(fisher, own, query)


def lane_groups(blocks, width):
    count, rows, lanes = blocks.shape
    if lanes == width:
        return blocks
    flat = jnp.swapaxes(blocks, 0, 1).reshape(rows, count * lanes)
    return jnp.swapaxes(flat.reshape(rows, -1, width), 0, 1)


def shift(x, axis, count, by):
    return lax.ppermute(x, axis, [(i, (i + by) % count) for i in range(count)])


def swap(x, axis, count, bit):
    return lax.ppermute(x, axis, [(i, i ^ bit) for i in range(count)])


def scatter_tokens(blocks, tensor):
    me = lax.axis_index("tensor")
    total = lax.dynamic_index_in_dim(blocks, me, 0, keepdims=False)
    for by in range(1, tensor):
        sent = lax.dynamic_index_in_dim(blocks, lax.rem(me + by, tensor), 0, keepdims=False)
        total = total + shift(sent, "tensor", tensor, by)
    return total


def gather_tokens(own, dp, tensor):
    if dp != 4 or tensor != 4:
        return lax.all_gather(own, ("dp", "tensor"))
    out = []
    for bit in range(4):
        here = own if bit == 0 else swap(own, "tensor", tensor, bit)
        across = swap(here, "dp", dp, 2)
        out += [here, across, swap(here, "dp", dp, 1), swap(across, "dp", dp, 1)]
    return jnp.stack(out)


def local(dp, tensor, acts, out_grads, proj_in, proj_out, query_acts, query_grads):
    tensor_index = lax.axis_index("tensor")
    dp_index = lax.axis_index("dp")
    cols = lambda proj, index, width: lax.dynamic_slice_in_dim(proj, index * width, width, 1)
    query = project(
        query_acts,
        query_grads,
        cols(proj_in, dp_index, query_acts.shape[1]),
        cols(proj_out, dp_index, query_grads.shape[1]),
        QLEN,
        LANES,
    )
    query = lax.psum(query, "dp")
    query = lane_groups(lax.all_gather(query, "tensor", axis=0, tiled=True), LANES)
    train = project(
        acts,
        out_grads,
        cols(proj_in, tensor_index, acts.shape[1]),
        cols(proj_out, tensor_index, out_grads.shape[1]),
        SEQ,
        256,
    )
    examples = train.shape[0] * LANES // tensor
    own = scatter_tokens(lane_groups(train, examples), tensor)
    every = lane_groups(gather_tokens(own, dp, tensor), LANES)
    fisher = gram(every)
    padded = jnp.pad(own, ((0, 0), (0, LANES - examples)))
    return solve(fisher, padded, query)[:examples]


def solution(mesh):
    in_specs = (
        P(("groups", "dp"), "tensor"),
        P(("groups", "dp"), "tensor"),
        P(),
        P(),
        P(("groups", "tensor"), "dp"),
        P(("groups", "tensor"), "dp"),
    )
    out_specs = P(("groups", "dp", "tensor"), None)
    body = functools.partial(local, mesh.shape["dp"], mesh.shape["tensor"])
    return jax.shard_map(body, mesh=mesh, in_specs=in_specs, out_specs=out_specs, check_vma=False)
```

```python
import functools

import jax
import jax.numpy as jnp
from jax import lax
from jax.experimental import pallas as pl
from jax.experimental.pallas import tpu as pltpu
from jax.sharding import PartitionSpec as P

SEQ = 8
QLEN = 4
RANK = 32
SIZE = RANK * RANK
LANES = 128
TILE = 128
BLOCKS = SIZE // TILE
VMEM = 56 * 1024 * 1024
F32 = jnp.float32
BF16 = jnp.bfloat16
TN = (((0,), (0,)), ((), ()))
NT = (((1,), (1,)), ((), ()))


def project_kernel(length, place_ref, ins_ref, outs_ref, pin_ref, pout_ref, o_ref, rows_ref, win_ref, wout_ref):
    step = pl.program_id(0)
    rows = ins_ref.shape[0]

    @pl.when(step == 0)
    def _():
        win_ref[...] = jnp.zeros_like(win_ref)
        wout_ref[...] = jnp.zeros_like(wout_ref)
        win_ref[RANK : 2 * RANK, :] = pin_ref[...]
        wout_ref[:RANK, :] = pout_ref[...]

    value = lax.dot_general(outs_ref[...], wout_ref[...], NT, preferred_element_type=F32)
    value += lax.dot_general(ins_ref[...], win_ref[...], NT, preferred_element_type=F32)
    rows_ref[pl.ds(pl.multiple_of(step * rows, rows), rows), :] = value

    @pl.when(step == pl.num_programs(0) - 1)
    def _():
        for t in range(length):
            o_ref[t * 2 * RANK : (t + 1) * 2 * RANK, :] = rows_ref[pl.ds(t, o_ref.shape[1], stride=length), :].T[
                : 2 * RANK
            ]


def project(ins, outs, proj_in, proj_out, length, tokens, rows, place, at):
    rows = min(rows, tokens)
    steps = tokens // rows
    examples = tokens // length
    widths = (ins.shape[1], outs.shape[1])
    grid_spec = pltpu.PrefetchScalarGridSpec(
        num_scalar_prefetch=1,
        grid=(steps,),
        in_specs=[pl.BlockSpec((rows, w), lambda i, place: (place[at] * steps + i, 0)) for w in widths]
        + [pl.BlockSpec((RANK, w), lambda i, place: (0, place[at + 1])) for w in widths],
        out_specs=pl.BlockSpec((length * 2 * RANK, examples), lambda i, place: (0, 0)),
        scratch_shapes=[pltpu.VMEM((tokens, LANES), F32)] + [pltpu.VMEM((LANES, w), BF16) for w in widths],
    )
    return pl.pallas_call(
        functools.partial(project_kernel, length),
        out_shape=jax.ShapeDtypeStruct((length * 2 * RANK, examples), F32),
        grid_spec=grid_spec,
        compiler_params=pltpu.CompilerParams(vmem_limit_bytes=VMEM),
        cost_estimate=pl.CostEstimate(
            flops=2 * tokens * sum(widths) * LANES, bytes_accessed=2 * tokens * sum(widths), transcendentals=0
        ),
    )(place, ins, outs, proj_in, proj_out)


def outer_rows(tok, length, a):
    total = None
    for t in range(length):
        base = t * 2 * RANK
        term = tok[base + a : base + a + 1, :] * tok[base + RANK : base + 2 * RANK, :]
        total = term if total is None else total + term
    return total


def split2(x):
    hi = x.astype(BF16)
    return hi, (x - hi.astype(F32)).astype(BF16)


def split3(x):
    hi = x.astype(BF16)
    rest = x - hi.astype(F32)
    mid = rest.astype(BF16)
    return hi, mid, (rest - mid.astype(F32)).astype(BF16)


def build_pair(toks, h, hi_ref, lo_ref):
    for q in range(2):
        for a in range(RANK):
            hi, lo = split2(outer_rows(toks[2 * h + q], SEQ, a))
            row, at = slice(a * RANK, (a + 1) * RANK), slice(q * LANES, (q + 1) * LANES)
            hi_ref[h, row, at] = hi
            lo_ref[h, row, at] = lo


BIG = 256


def add_gram(f_ref, before, h, r, start, stop, hi_ref, lo_ref):
    rows, cols = slice(r, r + BIG), slice(start, stop)
    term = lax.dot_general(hi_ref[h, rows, :], hi_ref[h, cols, :], NT, preferred_element_type=F32)
    term += lax.dot_general(hi_ref[h, rows, :], lo_ref[h, cols, :], NT, preferred_element_type=F32)
    term += lax.dot_general(lo_ref[h, rows, :], hi_ref[h, cols, :], NT, preferred_element_type=F32)
    old = before if h == 0 else f_ref
    f_ref[rows, cols] = term if old is None else old[rows, cols] + term


GROUP = 8
PAIRS = GROUP // 2
GRAM_SCRATCH = [pltpu.VMEM((PAIRS, SIZE, 2 * LANES), BF16)] * 2


def gram_kernel(first, *refs):
    toks, (f_ref, hi_ref, lo_ref) = refs[:GROUP], refs[-3:]
    for h in range(PAIRS):
        build_pair(toks, h, hi_ref, lo_ref)
        for r in range(0, SIZE, BIG):
            add_gram(f_ref, None if first else refs[GROUP], h, r, r, SIZE, hi_ref, lo_ref)


def gram(toks, total):
    first = total is None
    vmem = pl.BlockSpec(memory_space=pltpu.VMEM)
    return pl.pallas_call(
        functools.partial(gram_kernel, first),
        out_shape=jax.ShapeDtypeStruct((SIZE, SIZE), F32),
        in_specs=[vmem] * (GROUP + (not first)),
        out_specs=vmem,
        scratch_shapes=GRAM_SCRATCH,
        compiler_params=pltpu.CompilerParams(vmem_limit_bytes=VMEM),
        cost_estimate=pl.CostEstimate(
            flops=6 * SIZE * SIZE * GROUP * LANES, bytes_accessed=4 * SIZE * SIZE, transcendentals=0
        ),
    )(*toks, *([] if first else [total]))


def lanes_of(x, k):
    return jnp.broadcast_to(x[:, k : k + 1], (8, LANES))


def row_of(x, j):
    return jnp.broadcast_to(x[j : j + 1, :], (8, LANES))


def pair_left(parts, axis):
    hi, mid, lo = parts
    return jnp.concatenate([hi, hi, mid, mid, hi, lo], axis=axis)


def pair_right(parts, axis):
    hi, mid, lo = parts
    return jnp.concatenate([hi, mid, hi, mid, lo, hi], axis=axis)


def inverse_factor(groups, between):
    lane = lax.broadcasted_iota(jnp.int32, (8, LANES), 1)
    sub = lax.broadcasted_iota(jnp.int32, (8, LANES), 0)
    groups = list(groups)
    count = len(groups)
    pivots = [None] * count
    for q in range(count // 2):
        base, top, low = 16 * q, 2 * q, 2 * q + 1
        panel = (lane >= base) & (lane < base + 16)
        near = range(low + 1, min(low + 3, count))
        far = range(low + 3, count)
        tops = [lanes_of(groups[top], base + k) for k in range(8)]
        lows = [lanes_of(groups[low], base + k) for k in range(16)]
        cols = {i: [lanes_of(groups[i], base + k) for k in range(16)] for i in near}
        for i in near:
            groups[i] = jnp.where(panel, 0.0, groups[i])
        upper = jnp.where(panel, jnp.where(lane == sub + base, 1.0, 0.0), groups[top])
        lower = jnp.where(panel, jnp.where(lane == sub + base + 8, 1.0, 0.0), groups[low])
        pivot = [jnp.zeros((8, LANES), F32)] * 2
        scale = [jnp.zeros((8, LANES), F32)] * 2
        for j in range(16):
            half, jj = divmod(j, 8)
            diag = row_of((lows if half else tops)[j], jj)
            inv = -1.0 / diag
            pivot[half] = jnp.where(sub == jj, diag, pivot[half])
            scale[half] = jnp.where(sub == jj, inv, scale[half])
            row = row_of(lower if half else upper, jj)
            if half:
                ahead = {k: row_of(lows[k], jj) for k in range(j + 1, 16)}
            else:
                ahead = {k: row_of(tops[k], jj) if k < 8 else row_of(lows[j], k - 8) for k in range(j + 1, 16)}
            mult = lows[j] * inv
            if half:
                mult = jnp.where(sub > jj, mult, 0.0)
            else:
                first = jnp.where(sub > jj, tops[j] * inv, 0.0)
                for k in range(j + 1, 8):
                    tops[k] = tops[k] + first * ahead[k]
                upper = upper + first * row
            for k in range(j + 1, 16):
                lows[k] = lows[k] + mult * ahead[k]
            lower = lower + mult * row
            for i in near:
                mult = cols[i][j] * inv
                for k in range(j + 1, 16):
                    cols[i][k] = cols[i][k] + mult * ahead[k]
                groups[i] = groups[i] + mult * row
        groups[top], groups[low] = upper, lower
        pivots[top], pivots[low] = pivot
        if len(far) > 0:
            left = pair_left(split3(jnp.concatenate([upper * scale[0], lower * scale[1]], axis=0)), 0)
            right = pair_right(split3(jnp.concatenate([upper, lower], axis=0)), 0)
            update = lax.dot_general(left, right, TN, preferred_element_type=F32)
            for i in far:
                groups[i] = jnp.where(panel, 0.0, groups[i]) + update[8 * i : 8 * i + 8]
        between(q)
    return [jnp.where(lane <= sub + 8 * p, groups[p], 0.0) * lax.rsqrt(pivots[p]) for p in range(count)]


def share(tasks, part, parts):
    for task in tasks[len(tasks) * part // parts : len(tasks) * (part + 1) // parts]:
        task()


def solve_kernel(*refs):
    toks, (before, own_ref, query_ref, o_ref, f_ref, r_ref, x_ref, y_ref, hi_ref, lo_ref) = refs[:GROUP], refs[GROUP:]
    width = r_ref.shape[1]
    for h in range(PAIRS):
        build_pair(toks, h, hi_ref, lo_ref)
        for r in range(0, SIZE, BIG):
            add_gram(f_ref, before, h, r, r, r + BIG, hi_ref, lo_ref)
    eye = lax.broadcasted_iota(jnp.int32, (TILE, TILE), 0) == lax.broadcasted_iota(jnp.int32, (TILE, TILE), 1)
    total = jnp.zeros((TILE, TILE), F32)
    for b in range(BLOCKS):
        rows = slice(b * TILE, (b + 1) * TILE)
        total += jnp.where(eye, f_ref[rows, rows], 0.0)
    damping = 0.1 / SIZE * jnp.sum(total)

    def gram_task(h, r):
        return lambda: add_gram(f_ref, before, h, r, r + BIG, SIZE, hi_ref, lo_ref)

    def right_task(a):
        def run():
            rows = slice(a * RANK, (a + 1) * RANK)
            r_ref[rows, :LANES] = outer_rows(own_ref, SEQ, a)
            for s in range(query_ref.shape[0]):
                r_ref[rows, (s + 1) * LANES : (s + 2) * LANES] = outer_rows(query_ref.at[s], QLEN, a)

        return run

    def keep(slot, at, w):
        parts = split3(w)
        cols = slice(at, at + w.shape[1])
        y_ref[slot, :, cols] = pair_right(parts, 0)
        wide = x_ref.shape[2]
        if at < wide:
            x_ref[slot, :, at : min(at + w.shape[1], wide)] = pair_left(parts, 0)[:, : wide - at]

    def times(left, right):
        return jnp.dot(left, pair_right(split3(right), 0), preferred_element_type=F32)

    def white_task(slot, rows, left, at, stop):
        def run():
            if at >= SIZE:
                keep(slot, at, times(left, r_ref[rows, at - SIZE : stop - SIZE]))
            else:
                keep(slot, at, times(left, f_ref[rows, at:stop]))

        return run

    def rest_task(slot, i, start):
        def run():
            mine = slice(i * TILE, (i + 1) * TILE)
            delta = lax.dot_general(x_ref[slot, :, mine], y_ref[slot, :, start:], TN, preferred_element_type=F32)
            if start < SIZE:
                f_ref[mine, start:] -= delta[:, : SIZE - start]
            r_ref[mine, :] -= delta[:, SIZE - start :]

        return run

    def score_task(slot, first):
        def run():
            term = lax.dot_general(
                x_ref[slot, :, SIZE:], y_ref[slot, :, SIZE + LANES :], TN, preferred_element_type=F32
            )
            o_ref[...] = term if first else o_ref[...] + term

        return run

    tasks = [gram_task(h, r) for r in range(0, SIZE - BIG, BIG) for h in range(PAIRS)]
    tasks += [right_task(a) for a in range(RANK)]
    for b in range(BLOCKS):
        slot = b % 2
        rows = slice(b * TILE, (b + 1) * TILE)
        after = (b + 1) * TILE
        block = f_ref[rows, rows] + jnp.where(eye, damping, 0.0)
        between = lambda q, tasks=tasks: share(tasks, q, TILE // 16)
        inv = inverse_factor([block[8 * p : 8 * p + 8] for p in range(TILE // 8)], between)
        left = pair_left(split3(jnp.concatenate(inv, axis=0)), 1)
        if b + 1 < BLOCKS:
            keep(slot, after, times(left, f_ref[rows, after : after + TILE]))
            near = slice(after, after + TILE)
            f_ref[near, near] -= lax.dot_general(
                x_ref[slot, :, near], y_ref[slot, :, near], TN, preferred_element_type=F32
            )
        edges = list(range(after + TILE, SIZE, 512)) + [SIZE, SIZE + LANES, SIZE + width]
        tasks = [white_task(slot, rows, left, lo, hi) for lo, hi in zip(edges, edges[1:])]
        for i in range(b + 1, BLOCKS):
            tasks.append(rest_task(slot, i, max(i, b + 2) * TILE))
        tasks.append(score_task(slot, b == 0))
    share(tasks, 0, 1)


def solve(toks, fisher, own, query):
    width = (1 + query.shape[0]) * LANES
    return pl.pallas_call(
        solve_kernel,
        out_shape=jax.ShapeDtypeStruct((LANES, width - LANES), F32),
        in_specs=[pl.BlockSpec(memory_space=pltpu.VMEM)] * (GROUP + 3),
        out_specs=pl.BlockSpec(memory_space=pltpu.VMEM),
        scratch_shapes=[
            pltpu.VMEM((SIZE, SIZE), F32),
            pltpu.VMEM((SIZE, width), F32),
            pltpu.VMEM((2, 6 * TILE, SIZE + LANES), BF16),
            pltpu.VMEM((2, 6 * TILE, SIZE + width), BF16),
        ]
        + GRAM_SCRATCH,
        compiler_params=pltpu.CompilerParams(vmem_limit_bytes=VMEM),
    )(*toks, fisher, own, query)


def shift(x, axis, count, by):
    return lax.ppermute(x, axis, [(i, (i + by) % count) for i in range(count)])


def swap(x, axis, count, bit):
    return lax.ppermute(x, axis, [(i, i ^ bit) for i in range(count)])


def halves(x, first):
    size = x.shape[0] // 2
    return (
        lax.dynamic_slice_in_dim(x, first * size, size, 0),
        lax.dynamic_slice_in_dim(x, (1 - first) * size, size, 0),
    )


def in_order(mine, other, bit):
    return jnp.where(bit == 0, jnp.concatenate([mine, other]), jnp.concatenate([other, mine]))


def gather_query(part, dp, tensor):
    if dp != 4 or tensor != 4:
        return lane_groups(lax.all_gather(lax.psum(part, "dp"), "tensor"))
    index = lax.axis_index("dp")
    core, chip = lax.rem(index, 2), lax.div(index, 2)
    keep, send = halves(part, core)
    part = keep + swap(send, "dp", dp, 1)
    keep, send = halves(part, chip)
    part = keep + swap(send, "dp", dp, 2)
    blocks = jnp.concatenate([part] + [swap(part, "tensor", tensor, bit) for bit in range(1, 4)], axis=1)
    blocks = in_order(blocks, swap(blocks, "dp", dp, 2), chip)
    blocks = in_order(blocks, swap(blocks, "dp", dp, 1), core)
    me = lax.axis_index("tensor")
    blocks = jnp.swapaxes(blocks.reshape(blocks.shape[0], 4, -1), 0, 1)
    return jnp.stack([lax.dynamic_index_in_dim(blocks, me ^ t, 0, keepdims=False) for t in range(4)])


def lane_groups(blocks):
    count, rows, lanes = blocks.shape
    flat = jnp.swapaxes(blocks, 0, 1).reshape(rows, count * lanes)
    return jnp.swapaxes(flat.reshape(rows, -1, LANES), 0, 1)


def spread(here, dp):
    across = swap(here, "dp", dp, 2)
    return [here, across, swap(here, "dp", dp, 1), swap(across, "dp", dp, 1)]


def gather_tokens(own, dp, tensor):
    if dp != 4 or tensor != 4 or own.shape[1] != LANES:
        every = lane_groups(lax.all_gather(own, ("dp", "tensor")))
        every = [every[i] for i in range(every.shape[0])]
        total = None
        for at in range(0, len(every) - GROUP, GROUP):
            total = gram(every[at : at + GROUP], total)
        return every[-GROUP:], total
    near, *far = [swap(own, "tensor", tensor, bit) for bit in (1, 2, 3)]
    total = gram(spread(own, dp) + spread(near, dp), None)
    total, *far = lax.optimization_barrier((total, *far))
    return spread(far[0], dp) + spread(far[1], dp), total


def local(dp, tensor, acts, out_grads, proj_in, proj_out, query_acts, query_grads):
    me = lax.axis_index("tensor")
    order = sorted(range(tensor), key=lambda i: -min(i, tensor - i))
    zero = jnp.zeros_like(me)
    place = [zero, lax.axis_index("dp")]
    for by in order:
        place += [lax.rem(me + by, tensor), me]
    place = jnp.stack(place).astype(jnp.int32)
    part = project(query_acts, query_grads, proj_in, proj_out, QLEN, query_acts.shape[0], 256, place, 0)
    query = gather_query(part, dp, tensor)
    tokens = acts.shape[0] // tensor
    own = None
    for at, by in enumerate(order):
        part = project(acts, out_grads, proj_in, proj_out, SEQ, tokens, 512, place, 2 + 2 * at)
        part = part if by == 0 else shift(part, "tensor", tensor, by)
        own = part if own is None else own + part
    examples = own.shape[1]
    toks, fisher = gather_tokens(own, dp, tensor)
    padded = jnp.pad(own, ((0, 0), (0, LANES - examples)))
    return solve(toks, fisher, padded, query)[:examples]


def solution(mesh):
    in_specs = (
        P(("groups", "dp"), "tensor"),
        P(("groups", "dp"), "tensor"),
        P(),
        P(),
        P(("groups", "tensor"), "dp"),
        P(("groups", "tensor"), "dp"),
    )
    out_specs = P(("groups", "dp", "tensor"), None)
    body = functools.partial(local, mesh.shape["dp"], mesh.shape["tensor"])
    return jax.shard_map(body, mesh=mesh, in_specs=in_specs, out_specs=out_specs, check_vma=False)
```

```python
import functools

import jax
import jax.numpy as jnp
from jax import lax
from jax.experimental import pallas as pl
from jax.experimental.pallas import tpu as pltpu
from jax.sharding import PartitionSpec as P

SEQ = 8
QLEN = 4
RANK = 32
SIZE = RANK * RANK
LANES = 128
TILE = 128
BLOCKS = SIZE // TILE
VMEM = 56 * 1024 * 1024
F32 = jnp.float32
BF16 = jnp.bfloat16
TN = (((0,), (0,)), ((), ()))
NT = (((1,), (1,)), ((), ()))


def project_kernel(length, chunks, place_ref, ins_ref, outs_ref, pin_ref, pout_ref, *refs):
    o_refs, (rows_ref, win_ref, wout_ref) = refs[:chunks], refs[chunks:]
    step = pl.program_id(0)
    steps = pl.num_programs(0) // chunks
    rows = ins_ref.shape[0]

    @pl.when(step == 0)
    def _():
        win_ref[...] = jnp.zeros_like(win_ref)
        wout_ref[...] = jnp.zeros_like(wout_ref)
        win_ref[RANK : 2 * RANK, :] = pin_ref[...]
        wout_ref[:RANK, :] = pout_ref[...]

    value = lax.dot_general(outs_ref[...], wout_ref[...], NT, preferred_element_type=F32)
    value += lax.dot_general(ins_ref[...], win_ref[...], NT, preferred_element_type=F32)
    rows_ref[pl.ds(pl.multiple_of(lax.rem(step, steps) * rows, rows), rows), :] = value
    for c, o_ref in enumerate(o_refs):

        @pl.when(step == (c + 1) * steps - 1)
        def _():
            for t in range(length):
                o_ref[t * 2 * RANK : (t + 1) * 2 * RANK, :] = rows_ref[
                    pl.ds(t, o_ref.shape[1], stride=length), :
                ].T[: 2 * RANK]


def project(ins, outs, proj_in, proj_out, length, tokens, rows, place, at, chunks):
    rows = min(rows, tokens)
    steps = tokens // rows
    examples = tokens // length
    widths = (ins.shape[1], outs.shape[1])
    shape = (length * 2 * RANK, examples)
    grid_spec = pltpu.PrefetchScalarGridSpec(
        num_scalar_prefetch=1,
        grid=(chunks * steps,),
        in_specs=[
            pl.BlockSpec((rows, w), lambda i, place: (place[at + i // steps] * steps + lax.rem(i, steps), 0))
            for w in widths
        ]
        + [pl.BlockSpec((RANK, w), lambda i, place: (0, place[at + chunks])) for w in widths],
        out_specs=[pl.BlockSpec(shape, lambda i, place: (0, 0))] * chunks,
        scratch_shapes=[pltpu.VMEM((tokens, LANES), F32)] + [pltpu.VMEM((LANES, w), BF16) for w in widths],
    )
    return pl.pallas_call(
        functools.partial(project_kernel, length, chunks),
        out_shape=[jax.ShapeDtypeStruct(shape, F32)] * chunks,
        grid_spec=grid_spec,
        compiler_params=pltpu.CompilerParams(vmem_limit_bytes=VMEM),
        cost_estimate=pl.CostEstimate(flops=1, bytes_accessed=1, transcendentals=0),
    )(place, ins, outs, proj_in, proj_out)


def outer_rows(tok, length, a):
    total = None
    for t in range(length):
        base = t * 2 * RANK
        term = tok[base + a : base + a + 1, :] * tok[base + RANK : base + 2 * RANK, :]
        total = term if total is None else total + term
    return total


def split2(x):
    hi = x.astype(BF16)
    return hi, (x - hi.astype(F32)).astype(BF16)


def split3(x):
    hi = x.astype(BF16)
    rest = x - hi.astype(F32)
    mid = rest.astype(BF16)
    return hi, mid, (rest - mid.astype(F32)).astype(BF16)


def build_pair(toks, h, hi_ref, lo_ref):
    for q in range(2):
        for a in range(RANK):
            hi, lo = split2(outer_rows(toks[2 * h + q], SEQ, a))
            row, at = slice(a * RANK, (a + 1) * RANK), slice(q * LANES, (q + 1) * LANES)
            hi_ref[h, row, at] = hi
            lo_ref[h, row, at] = lo


BIG = 256


def add_gram(f_ref, before, h, r, start, stop, hi_ref, lo_ref):
    rows, cols = slice(r, r + BIG), slice(start, stop)
    term = lax.dot_general(hi_ref[h, rows, :], hi_ref[h, cols, :], NT, preferred_element_type=F32)
    term += lax.dot_general(hi_ref[h, rows, :], lo_ref[h, cols, :], NT, preferred_element_type=F32)
    term += lax.dot_general(lo_ref[h, rows, :], hi_ref[h, cols, :], NT, preferred_element_type=F32)
    old = before if h == 0 else f_ref
    f_ref[rows, cols] = term if old is None else old[rows, cols] + term


def gram_scratch(count):
    return [pltpu.VMEM((count // 2, SIZE, 2 * LANES), BF16)] * 2


def gram_kernel(count, first, *refs):
    toks, (f_ref, hi_ref, lo_ref) = refs[:count], refs[-3:]
    for h in range(count // 2):
        build_pair(toks, h, hi_ref, lo_ref)
        for r in range(0, SIZE, BIG):
            add_gram(f_ref, None if first else refs[count], h, r, r, SIZE, hi_ref, lo_ref)


def gram(toks, total):
    first = total is None
    count = len(toks)
    vmem = pl.BlockSpec(memory_space=pltpu.VMEM)
    return pl.pallas_call(
        functools.partial(gram_kernel, count, first),
        out_shape=jax.ShapeDtypeStruct((SIZE, SIZE), F32),
        in_specs=[vmem] * (count + (not first)),
        out_specs=vmem,
        scratch_shapes=gram_scratch(count),
        compiler_params=pltpu.CompilerParams(vmem_limit_bytes=VMEM),
        cost_estimate=pl.CostEstimate(flops=1, bytes_accessed=1, transcendentals=0),
    )(*toks, *([] if first else [total]))


def lanes_of(x, k):
    return jnp.broadcast_to(x[:, k : k + 1], (8, LANES))


def row_of(x, j):
    return jnp.broadcast_to(x[j : j + 1, :], (8, LANES))


def pair_left(parts, axis):
    hi, mid, lo = parts
    return jnp.concatenate([hi, hi, mid, mid, hi, lo], axis=axis)


def pair_right(parts, axis):
    hi, mid, lo = parts
    return jnp.concatenate([hi, mid, hi, mid, lo, hi], axis=axis)


def inverse_factor(groups, between):
    lane = lax.broadcasted_iota(jnp.int32, (8, LANES), 1)
    sub = lax.broadcasted_iota(jnp.int32, (8, LANES), 0)
    groups = list(groups)
    count = len(groups)
    pivots = [None] * count
    for q in range(count // 2):
        base, top, low = 16 * q, 2 * q, 2 * q + 1
        panel = (lane >= base) & (lane < base + 16)
        near = range(low + 1, min(low + 3, count))
        far = range(low + 3, count)
        tops = [lanes_of(groups[top], base + k) for k in range(8)]
        lows = [lanes_of(groups[low], base + k) for k in range(16)]
        cols = {i: [lanes_of(groups[i], base + k) for k in range(16)] for i in near}
        for i in near:
            groups[i] = jnp.where(panel, 0.0, groups[i])
        upper = jnp.where(panel, jnp.where(lane == sub + base, 1.0, 0.0), groups[top])
        lower = jnp.where(panel, jnp.where(lane == sub + base + 8, 1.0, 0.0), groups[low])
        pivot = [jnp.zeros((8, LANES), F32)] * 2
        scale = [jnp.zeros((8, LANES), F32)] * 2
        for j in range(16):
            half, jj = divmod(j, 8)
            diag = row_of((lows if half else tops)[j], jj)
            inv = -1.0 / diag
            pivot[half] = jnp.where(sub == jj, diag, pivot[half])
            scale[half] = jnp.where(sub == jj, inv, scale[half])
            row = row_of(lower if half else upper, jj)
            if half:
                ahead = {k: row_of(lows[k], jj) for k in range(j + 1, 16)}
            else:
                ahead = {k: row_of(tops[k], jj) if k < 8 else row_of(lows[j], k - 8) for k in range(j + 1, 16)}
            mult = lows[j] * inv
            if half:
                mult = jnp.where(sub > jj, mult, 0.0)
            else:
                first = jnp.where(sub > jj, tops[j] * inv, 0.0)
                for k in range(j + 1, 8):
                    tops[k] = tops[k] + first * ahead[k]
                upper = upper + first * row
            for k in range(j + 1, 16):
                lows[k] = lows[k] + mult * ahead[k]
            lower = lower + mult * row
            for i in near:
                mult = cols[i][j] * inv
                for k in range(j + 1, 16):
                    cols[i][k] = cols[i][k] + mult * ahead[k]
                groups[i] = groups[i] + mult * row
        groups[top], groups[low] = upper, lower
        pivots[top], pivots[low] = pivot
        if len(far) > 0:
            left = pair_left(split3(jnp.concatenate([upper * scale[0], lower * scale[1]], axis=0)), 0)
            right = pair_right(split3(jnp.concatenate([upper, lower], axis=0)), 0)
            update = lax.dot_general(left, right, TN, preferred_element_type=F32)
            for i in far:
                groups[i] = jnp.where(panel, 0.0, groups[i]) + update[8 * i : 8 * i + 8]
        between(q)
    return [jnp.where(lane <= sub + 8 * p, groups[p], 0.0) * lax.rsqrt(pivots[p]) for p in range(count)]


def share(tasks, part, parts):
    for task in tasks[len(tasks) * part // parts : len(tasks) * (part + 1) // parts]:
        task()


def solve_kernel(count, *refs):
    toks, (before, own_ref, query_ref, o_ref, f_ref, r_ref, x_ref, y_ref, hi_ref, lo_ref) = refs[:count], refs[count:]
    pairs = count // 2
    width = r_ref.shape[1]
    for h in range(pairs):
        build_pair(toks, h, hi_ref, lo_ref)
        for r in range(0, SIZE, BIG):
            add_gram(f_ref, before, h, r, r, r + BIG, hi_ref, lo_ref)
    eye = lax.broadcasted_iota(jnp.int32, (TILE, TILE), 0) == lax.broadcasted_iota(jnp.int32, (TILE, TILE), 1)
    total = jnp.zeros((TILE, TILE), F32)
    for b in range(BLOCKS):
        rows = slice(b * TILE, (b + 1) * TILE)
        total += jnp.where(eye, f_ref[rows, rows], 0.0)
    damping = 0.1 / SIZE * jnp.sum(total)

    def gram_task(h, r):
        return lambda: add_gram(f_ref, before, h, r, r + BIG, SIZE, hi_ref, lo_ref)

    def right_task(a):
        def run():
            rows = slice(a * RANK, (a + 1) * RANK)
            r_ref[rows, :LANES] = outer_rows(own_ref, SEQ, a)
            for s in range(query_ref.shape[0]):
                r_ref[rows, (s + 1) * LANES : (s + 2) * LANES] = outer_rows(query_ref.at[s], QLEN, a)

        return run

    def keep(slot, at, w):
        parts = split3(w)
        cols = slice(at, at + w.shape[1])
        y_ref[slot, :, cols] = pair_right(parts, 0)
        wide = x_ref.shape[2]
        if at < wide:
            x_ref[slot, :, at : min(at + w.shape[1], wide)] = pair_left(parts, 0)[:, : wide - at]

    def times(left, right):
        return jnp.dot(left, pair_right(split3(right), 0), preferred_element_type=F32)

    def white_task(slot, rows, left, at, stop):
        def run():
            if at >= SIZE:
                keep(slot, at, times(left, r_ref[rows, at - SIZE : stop - SIZE]))
            else:
                keep(slot, at, times(left, f_ref[rows, at:stop]))

        return run

    def rest_task(slot, i, start):
        def run():
            mine = slice(i * TILE, (i + 1) * TILE)
            delta = lax.dot_general(x_ref[slot, :, mine], y_ref[slot, :, start:], TN, preferred_element_type=F32)
            if start < SIZE:
                f_ref[mine, start:] -= delta[:, : SIZE - start]
            r_ref[mine, :] -= delta[:, SIZE - start :]

        return run

    def score_task(slot, first):
        def run():
            term = lax.dot_general(
                x_ref[slot, :, SIZE:], y_ref[slot, :, SIZE + LANES :], TN, preferred_element_type=F32
            )
            o_ref[...] = term if first else o_ref[...] + term

        return run

    tasks = [gram_task(h, r) for r in range(0, SIZE - BIG, BIG) for h in range(pairs)]
    tasks += [right_task(a) for a in range(RANK)]
    for b in range(BLOCKS):
        slot = b % 2
        rows = slice(b * TILE, (b + 1) * TILE)
        after = (b + 1) * TILE
        block = f_ref[rows, rows] + jnp.where(eye, damping, 0.0)
        between = lambda q, tasks=tasks: share(tasks, q, TILE // 16)
        inv = inverse_factor([block[8 * p : 8 * p + 8] for p in range(TILE // 8)], between)
        left = pair_left(split3(jnp.concatenate(inv, axis=0)), 1)
        if b + 1 < BLOCKS:
            keep(slot, after, times(left, f_ref[rows, after : after + TILE]))
            near = slice(after, after + TILE)
            f_ref[near, near] -= lax.dot_general(
                x_ref[slot, :, near], y_ref[slot, :, near], TN, preferred_element_type=F32
            )
        edges = list(range(after + TILE, SIZE, 512)) + [SIZE, SIZE + LANES, SIZE + width]
        tasks = [white_task(slot, rows, left, lo, hi) for lo, hi in zip(edges, edges[1:])]
        for i in range(b + 1, BLOCKS):
            tasks.append(rest_task(slot, i, max(i, b + 2) * TILE))
        tasks.append(score_task(slot, b == 0))
    share(tasks, 0, 1)


def solve(toks, fisher, own, query):
    width = (1 + query.shape[0]) * LANES
    return pl.pallas_call(
        functools.partial(solve_kernel, len(toks)),
        out_shape=jax.ShapeDtypeStruct((LANES, width - LANES), F32),
        in_specs=[pl.BlockSpec(memory_space=pltpu.VMEM)] * (len(toks) + 3),
        out_specs=pl.BlockSpec(memory_space=pltpu.VMEM),
        scratch_shapes=[
            pltpu.VMEM((SIZE, SIZE), F32),
            pltpu.VMEM((SIZE, width), F32),
            pltpu.VMEM((2, 6 * TILE, SIZE + LANES), BF16),
            pltpu.VMEM((2, 6 * TILE, SIZE + width), BF16),
        ]
        + gram_scratch(len(toks)),
        compiler_params=pltpu.CompilerParams(vmem_limit_bytes=VMEM),
    )(*toks, fisher, own, query)


def shift(x, axis, count, by):
    return lax.ppermute(x, axis, [(i, (i + by) % count) for i in range(count)])


def swap(x, axis, count, bit):
    return lax.ppermute(x, axis, [(i, i ^ bit) for i in range(count)])


def halves(x, first):
    size = x.shape[0] // 2
    return (
        lax.dynamic_slice_in_dim(x, first * size, size, 0),
        lax.dynamic_slice_in_dim(x, (1 - first) * size, size, 0),
    )


def in_order(mine, other, bit):
    return jnp.where(bit == 0, jnp.concatenate([mine, other]), jnp.concatenate([other, mine]))


def lane_groups(blocks):
    count, rows, lanes = blocks.shape
    flat = jnp.swapaxes(blocks, 0, 1).reshape(rows, count * lanes)
    return jnp.swapaxes(flat.reshape(rows, -1, LANES), 0, 1)


def after(value, *earlier):
    return lax.optimization_barrier((value, earlier))[0]


def both_cores(pair):
    return pair + [swap(x, "dp", 4, 1) for x in pair]


def square(train, query, place):
    me = lax.axis_index("tensor")
    core, chip = lax.rem(lax.axis_index("dp"), 2), lax.div(lax.axis_index("dp"), 2)
    part = train(2, place)
    two = shift(part, "tensor", 4, 2)
    asked = query(after(place, part))
    keep, send = halves(asked, core)
    other = swap(send, "dp", 4, 1)
    part = train(1, after(place, asked))
    one = shift(part, "tensor", 4, 1)
    place = after(place, part, two, other)
    keep, send = halves(keep + other, chip)
    other = swap(send, "dp", 4, 2)
    part = train(3, place)
    three = shift(part, "tensor", 4, 3)
    own = after(train(0, after(place, part, one)), other) + two + one + three

    near, far, across = swap(own, "tensor", 4, 1), swap(own, "tensor", 4, 2), swap(own, "dp", 4, 2)
    near = after(near, across)
    near_across = swap(near, "dp", 4, 2)
    asked = after(keep + other, near)
    asked = jnp.concatenate([asked] + [swap(asked, "tensor", 4, bit) for bit in (1, 2, 3)], axis=1)
    far = after(far, near_across)
    last = swap(after(own, far), "tensor", 4, 3)
    far = [far, swap(far, "dp", 4, 2)]
    asked = after(asked, far[0])
    blocks = in_order(asked, swap(asked, "dp", 4, 2), chip)
    total = gram(after(both_cores([own, across]), far[0]), None)
    last, far, blocks = after([last, far, blocks], total)
    last_across = swap(last, "dp", 4, 2)
    total = gram(after(both_cores([near, near_across]), last), total)
    last_across = after(last_across, total)
    blocks = in_order(blocks, swap(blocks, "dp", 4, 1), core)
    blocks = jnp.swapaxes(blocks.reshape(blocks.shape[0], 4, -1), 0, 1)
    asked = jnp.stack([lax.dynamic_index_in_dim(blocks, me ^ t, 0, keepdims=False) for t in range(4)])
    return own, both_cores(far) + both_cores([last, last_across]), total, asked


def anywhere(train, query, place, dp, tensor):
    asked = lane_groups(lax.all_gather(lax.psum(query(place), "dp"), "tensor"))
    own = train(0, place)
    for by in range(1, tensor):
        own = own + shift(train(by, place), "tensor", tensor, by)
    every = lane_groups(lax.all_gather(own, ("dp", "tensor")))
    every = [every[i] for i in range(every.shape[0])]
    total = None
    for at in range(0, len(every) - 8, 8):
        total = gram(every[at : at + 8], total)
    return own, every[-8:], total, asked


def local(dp, tensor, acts, out_grads, proj_in, proj_out, query_acts, query_grads):
    me = lax.axis_index("tensor")
    place = [jnp.zeros_like(me), lax.axis_index("dp")]
    for by in range(tensor):
        place += [lax.rem(me + by, tensor), me]
    place = jnp.stack(place).astype(jnp.int32)
    tokens = acts.shape[0] // tensor

    def train(by, place):
        return project(acts, out_grads, proj_in, proj_out, SEQ, tokens, 512, place, 2 + 2 * by, 1)[0]

    def query(place):
        return project(query_acts, query_grads, proj_in, proj_out, QLEN, query_acts.shape[0], 256, place, 0, 1)[0]

    if dp == 4 and tensor == 4 and tokens == SEQ * LANES:
        own, toks, total, asked = square(train, query, place)
    else:
        own, toks, total, asked = anywhere(train, query, place, dp, tensor)
    examples = own.shape[1]
    padded = jnp.pad(own, ((0, 0), (0, LANES - examples)))
    return solve(toks, total, padded, asked)[:examples]


def solution(mesh):
    in_specs = (
        P(("groups", "dp"), "tensor"),
        P(("groups", "dp"), "tensor"),
        P(),
        P(),
        P(("groups", "tensor"), "dp"),
        P(("groups", "tensor"), "dp"),
    )
    out_specs = P(("groups", "dp", "tensor"), None)
    body = functools.partial(local, mesh.shape["dp"], mesh.shape["tensor"])
    return jax.shard_map(body, mesh=mesh, in_specs=in_specs, out_specs=out_specs, check_vma=False)
```

```python
import functools

import jax
import jax.numpy as jnp
from jax import lax
from jax.experimental import pallas as pl
from jax.experimental.pallas import tpu as pltpu
from jax.sharding import PartitionSpec as P

SEQ = 8
QLEN = 4
RANK = 32
SIZE = RANK * RANK
LANES = 128
TILE = 128
BLOCKS = SIZE // TILE
VMEM = 56 * 1024 * 1024
F32 = jnp.float32
BF16 = jnp.bfloat16
TN = (((0,), (0,)), ((), ()))
NT = (((1,), (1,)), ((), ()))


def project_kernel(length, chunks, place_ref, ins_ref, outs_ref, pin_ref, pout_ref, *refs):
    o_refs, (rows_ref, win_ref, wout_ref) = refs[:chunks], refs[chunks:]
    step = pl.program_id(0)
    steps = pl.num_programs(0) // chunks
    rows = ins_ref.shape[0]

    @pl.when(step == 0)
    def _():
        win_ref[...] = jnp.zeros_like(win_ref)
        wout_ref[...] = jnp.zeros_like(wout_ref)
        win_ref[RANK : 2 * RANK, :] = pin_ref[...]
        wout_ref[:RANK, :] = pout_ref[...]

    value = lax.dot_general(outs_ref[...], wout_ref[...], NT, preferred_element_type=F32)
    value += lax.dot_general(ins_ref[...], win_ref[...], NT, preferred_element_type=F32)
    rows_ref[pl.ds(pl.multiple_of(lax.rem(step, steps) * rows, rows), rows), :] = value
    for c, o_ref in enumerate(o_refs):

        @pl.when(step == (c + 1) * steps - 1)
        def _():
            for t in range(length):
                o_ref[t * 2 * RANK : (t + 1) * 2 * RANK, :] = rows_ref[
                    pl.ds(t, o_ref.shape[1], stride=length), :
                ].T[: 2 * RANK]


def project(ins, outs, proj_in, proj_out, length, tokens, rows, place, at, chunks):
    rows = min(rows, tokens)
    steps = tokens // rows
    examples = tokens // length
    widths = (ins.shape[1], outs.shape[1])
    shape = (length * 2 * RANK, examples)
    grid_spec = pltpu.PrefetchScalarGridSpec(
        num_scalar_prefetch=1,
        grid=(chunks * steps,),
        in_specs=[
            pl.BlockSpec((rows, w), lambda i, place: (place[at + i // steps] * steps + lax.rem(i, steps), 0))
            for w in widths
        ]
        + [pl.BlockSpec((RANK, w), lambda i, place: (0, place[at + chunks])) for w in widths],
        out_specs=[pl.BlockSpec(shape, lambda i, place: (0, 0))] * chunks,
        scratch_shapes=[pltpu.VMEM((tokens, LANES), F32)] + [pltpu.VMEM((LANES, w), BF16) for w in widths],
    )
    return pl.pallas_call(
        functools.partial(project_kernel, length, chunks),
        out_shape=[jax.ShapeDtypeStruct(shape, F32)] * chunks,
        grid_spec=grid_spec,
        compiler_params=pltpu.CompilerParams(vmem_limit_bytes=VMEM),
        cost_estimate=pl.CostEstimate(flops=1, bytes_accessed=1, transcendentals=0),
    )(place, ins, outs, proj_in, proj_out)


def outer_rows(tok, length, a):
    total = None
    for t in range(length):
        base = t * 2 * RANK
        term = tok[base + a : base + a + 1, :] * tok[base + RANK : base + 2 * RANK, :]
        total = term if total is None else total + term
    return total


def split2(x):
    hi = x.astype(BF16)
    return hi, (x - hi.astype(F32)).astype(BF16)


def split3(x):
    hi = x.astype(BF16)
    rest = x - hi.astype(F32)
    mid = rest.astype(BF16)
    return hi, mid, (rest - mid.astype(F32)).astype(BF16)


def build_pair(toks, h, hi_ref, lo_ref):
    for q in range(2):
        for a in range(RANK):
            hi, lo = split2(outer_rows(toks[2 * h + q], SEQ, a))
            row, at = slice(a * RANK, (a + 1) * RANK), slice(q * LANES, (q + 1) * LANES)
            hi_ref[h, row, at] = hi
            lo_ref[h, row, at] = lo


BIG = 256


def add_gram(f_ref, before, h, r, start, stop, hi_ref, lo_ref):
    rows, cols = slice(r, r + BIG), slice(start, stop)
    term = lax.dot_general(hi_ref[h, rows, :], hi_ref[h, cols, :], NT, preferred_element_type=F32)
    term += lax.dot_general(hi_ref[h, rows, :], lo_ref[h, cols, :], NT, preferred_element_type=F32)
    term += lax.dot_general(lo_ref[h, rows, :], hi_ref[h, cols, :], NT, preferred_element_type=F32)
    old = before if h == 0 else f_ref
    f_ref[rows, cols] = term if old is None else old[rows, cols] + term


def gram_scratch(count):
    return [pltpu.VMEM((count // 2, SIZE, 2 * LANES), BF16)] * 2


def gram_kernel(count, first, *refs):
    toks, (f_ref, hi_ref, lo_ref) = refs[:count], refs[-3:]
    for h in range(count // 2):
        build_pair(toks, h, hi_ref, lo_ref)
        for r in range(0, SIZE, BIG):
            add_gram(f_ref, None if first else refs[count], h, r, r, SIZE, hi_ref, lo_ref)


def gram(toks, total):
    first = total is None
    count = len(toks)
    vmem = pl.BlockSpec(memory_space=pltpu.VMEM)
    return pl.pallas_call(
        functools.partial(gram_kernel, count, first),
        out_shape=jax.ShapeDtypeStruct((SIZE, SIZE), F32),
        in_specs=[vmem] * (count + (not first)),
        out_specs=vmem,
        scratch_shapes=gram_scratch(count),
        compiler_params=pltpu.CompilerParams(vmem_limit_bytes=VMEM),
        cost_estimate=pl.CostEstimate(flops=1, bytes_accessed=1, transcendentals=0),
    )(*toks, *([] if first else [total]))


def lanes_of(x, k):
    return jnp.broadcast_to(x[:, k : k + 1], (8, LANES))


def row_of(x, j):
    return jnp.broadcast_to(x[j : j + 1, :], (8, LANES))


def pair_left(parts, axis):
    hi, mid, lo = parts
    return jnp.concatenate([hi, hi, mid, mid, hi, lo], axis=axis)


def pair_right(parts, axis):
    hi, mid, lo = parts
    return jnp.concatenate([hi, mid, hi, mid, lo, hi], axis=axis)


def inverse_factor(groups, between):
    lane = lax.broadcasted_iota(jnp.int32, (8, LANES), 1)
    sub = lax.broadcasted_iota(jnp.int32, (8, LANES), 0)
    groups = list(groups)
    count = len(groups)
    pivots = [None] * count
    for q in range(count // 2):
        base, top, low = 16 * q, 2 * q, 2 * q + 1
        panel = (lane >= base) & (lane < base + 16)
        near = range(low + 1, min(low + 3, count))
        far = range(low + 3, count)
        tops = [lanes_of(groups[top], base + k) for k in range(8)]
        lows = [lanes_of(groups[low], base + k) for k in range(16)]
        cols = {i: [lanes_of(groups[i], base + k) for k in range(16)] for i in near}
        for i in near:
            groups[i] = jnp.where(panel, 0.0, groups[i])
        upper = jnp.where(panel, jnp.where(lane == sub + base, 1.0, 0.0), groups[top])
        lower = jnp.where(panel, jnp.where(lane == sub + base + 8, 1.0, 0.0), groups[low])
        pivot = [jnp.zeros((8, LANES), F32)] * 2
        scale = [jnp.zeros((8, LANES), F32)] * 2
        for j in range(16):
            half, jj = divmod(j, 8)
            diag = row_of((lows if half else tops)[j], jj)
            inv = -1.0 / diag
            pivot[half] = jnp.where(sub == jj, diag, pivot[half])
            scale[half] = jnp.where(sub == jj, inv, scale[half])
            row = row_of(lower if half else upper, jj)
            if half:
                ahead = {k: row_of(lows[k], jj) for k in range(j + 1, 16)}
            else:
                ahead = {k: row_of(tops[k], jj) if k < 8 else row_of(lows[j], k - 8) for k in range(j + 1, 16)}
            mult = lows[j] * inv
            if half:
                mult = jnp.where(sub > jj, mult, 0.0)
            else:
                first = jnp.where(sub > jj, tops[j] * inv, 0.0)
                for k in range(j + 1, 8):
                    tops[k] = tops[k] + first * ahead[k]
                upper = upper + first * row
            for k in range(j + 1, 16):
                lows[k] = lows[k] + mult * ahead[k]
            lower = lower + mult * row
            for i in near:
                mult = cols[i][j] * inv
                for k in range(j + 1, 16):
                    cols[i][k] = cols[i][k] + mult * ahead[k]
                groups[i] = groups[i] + mult * row
        groups[top], groups[low] = upper, lower
        pivots[top], pivots[low] = pivot
        if len(far) > 0:
            left = pair_left(split3(jnp.concatenate([upper * scale[0], lower * scale[1]], axis=0)), 0)
            right = pair_right(split3(jnp.concatenate([upper, lower], axis=0)), 0)
            update = lax.dot_general(left, right, TN, preferred_element_type=F32)
            for i in far:
                groups[i] = jnp.where(panel, 0.0, groups[i]) + update[8 * i : 8 * i + 8]
        between(q)
    return [jnp.where(lane <= sub + 8 * p, groups[p], 0.0) * lax.rsqrt(pivots[p]) for p in range(count)]


def share(tasks, part, parts):
    for task in tasks[len(tasks) * part // parts : len(tasks) * (part + 1) // parts]:
        task()


def solve_kernel(count, *refs):
    toks, (before, own_ref, query_ref, order_ref, o_ref, f_ref, r_ref, x_ref, y_ref, hi_ref, lo_ref) = refs[:count], refs[count:]
    pairs = count // 2
    width = r_ref.shape[1]
    for h in range(pairs):
        build_pair(toks, h, hi_ref, lo_ref)
        for r in range(0, SIZE, BIG):
            add_gram(f_ref, before, h, r, r, r + BIG, hi_ref, lo_ref)
    eye = lax.broadcasted_iota(jnp.int32, (TILE, TILE), 0) == lax.broadcasted_iota(jnp.int32, (TILE, TILE), 1)
    total = jnp.zeros((TILE, TILE), F32)
    for b in range(BLOCKS):
        rows = slice(b * TILE, (b + 1) * TILE)
        total += jnp.where(eye, f_ref[rows, rows], 0.0)
    damping = 0.1 / SIZE * jnp.sum(total)

    def gram_task(h, r):
        return lambda: add_gram(f_ref, before, h, r, r + BIG, SIZE, hi_ref, lo_ref)

    def right_task(a):
        def run():
            rows = slice(a * RANK, (a + 1) * RANK)
            r_ref[rows, :LANES] = outer_rows(own_ref, SEQ, a)
            for s in range(query_ref.shape[1] // LANES):
                block = query_ref.at[:, pl.ds(pl.multiple_of(order_ref[s] * LANES, LANES), LANES)]
                r_ref[rows, (s + 1) * LANES : (s + 2) * LANES] = outer_rows(block, QLEN, a)

        return run

    def keep(slot, at, w):
        parts = split3(w)
        cols = slice(at, at + w.shape[1])
        y_ref[slot, :, cols] = pair_right(parts, 0)
        wide = x_ref.shape[2]
        if at < wide:
            x_ref[slot, :, at : min(at + w.shape[1], wide)] = pair_left(parts, 0)[:, : wide - at]

    def times(left, right):
        return jnp.dot(left, pair_right(split3(right), 0), preferred_element_type=F32)

    def white_task(slot, rows, left, at, stop):
        def run():
            if at >= SIZE:
                keep(slot, at, times(left, r_ref[rows, at - SIZE : stop - SIZE]))
            else:
                keep(slot, at, times(left, f_ref[rows, at:stop]))

        return run

    def rest_task(slot, i, start):
        def run():
            mine = slice(i * TILE, (i + 1) * TILE)
            delta = lax.dot_general(x_ref[slot, :, mine], y_ref[slot, :, start:], TN, preferred_element_type=F32)
            if start < SIZE:
                f_ref[mine, start:] -= delta[:, : SIZE - start]
            r_ref[mine, :] -= delta[:, SIZE - start :]

        return run

    def score_task(slot, first):
        def run():
            term = lax.dot_general(
                x_ref[slot, :, SIZE:], y_ref[slot, :, SIZE + LANES :], TN, preferred_element_type=F32
            )
            o_ref[...] = term if first else o_ref[...] + term

        return run

    tasks = [gram_task(h, r) for r in range(0, SIZE - BIG, BIG) for h in range(pairs)]
    tasks += [right_task(a) for a in range(RANK)]
    for b in range(BLOCKS):
        slot = b % 2
        rows = slice(b * TILE, (b + 1) * TILE)
        after = (b + 1) * TILE
        block = f_ref[rows, rows] + jnp.where(eye, damping, 0.0)
        between = lambda q, tasks=tasks: share(tasks, q, TILE // 16)
        inv = inverse_factor([block[8 * p : 8 * p + 8] for p in range(TILE // 8)], between)
        left = pair_left(split3(jnp.concatenate(inv, axis=0)), 1)
        if b + 1 < BLOCKS:
            keep(slot, after, times(left, f_ref[rows, after : after + TILE]))
            near = slice(after, after + TILE)
            f_ref[near, near] -= lax.dot_general(
                x_ref[slot, :, near], y_ref[slot, :, near], TN, preferred_element_type=F32
            )
        edges = list(range(after + TILE, SIZE, 512)) + [SIZE, SIZE + LANES, SIZE + width]
        tasks = [white_task(slot, rows, left, lo, hi) for lo, hi in zip(edges, edges[1:])]
        for i in range(b + 1, BLOCKS):
            tasks.append(rest_task(slot, i, max(i, b + 2) * TILE))
        tasks.append(score_task(slot, b == 0))
    share(tasks, 0, 1)


def solve(toks, fisher, own, query, order):
    width = LANES + query.shape[1]
    return pl.pallas_call(
        functools.partial(solve_kernel, len(toks)),
        out_shape=jax.ShapeDtypeStruct((LANES, width - LANES), F32),
        in_specs=[pl.BlockSpec(memory_space=pltpu.VMEM)] * (len(toks) + 3) + [pl.BlockSpec(memory_space=pltpu.SMEM)],
        out_specs=pl.BlockSpec(memory_space=pltpu.VMEM),
        scratch_shapes=[
            pltpu.VMEM((SIZE, SIZE), F32),
            pltpu.VMEM((SIZE, width), F32),
            pltpu.VMEM((2, 6 * TILE, SIZE + LANES), BF16),
            pltpu.VMEM((2, 6 * TILE, SIZE + width), BF16),
        ]
        + gram_scratch(len(toks)),
        compiler_params=pltpu.CompilerParams(vmem_limit_bytes=VMEM),
    )(*toks, fisher, own, query, order)


def shift(x, axis, count, by):
    return lax.ppermute(x, axis, [(i, (i + by) % count) for i in range(count)])


def swap(x, axis, count, bit):
    return lax.ppermute(x, axis, [(i, i ^ bit) for i in range(count)])


def halves(x, first):
    size = x.shape[0] // 2
    return (
        lax.dynamic_slice_in_dim(x, first * size, size, 0),
        lax.dynamic_slice_in_dim(x, (1 - first) * size, size, 0),
    )


def in_order(mine, other, bit):
    return jnp.where(bit == 0, jnp.concatenate([mine, other]), jnp.concatenate([other, mine]))


def lane_groups(blocks):
    count, rows, lanes = blocks.shape
    flat = jnp.swapaxes(blocks, 0, 1).reshape(rows, count * lanes)
    return jnp.swapaxes(flat.reshape(rows, -1, LANES), 0, 1)


def after(value, *earlier):
    return lax.optimization_barrier((value, earlier))[0]


def both_cores(pair):
    return pair + [swap(x, "dp", 4, 1) for x in pair]


def square(train, query, place):
    me = lax.axis_index("tensor")
    core, chip = lax.rem(lax.axis_index("dp"), 2), lax.div(lax.axis_index("dp"), 2)
    part = train(2, place)
    two = shift(part, "tensor", 4, 2)
    asked = query(after(place, part))
    keep, send = halves(asked, core)
    other = swap(send, "dp", 4, 1)
    part = train(1, after(place, asked))
    one = shift(part, "tensor", 4, 1)
    place = after(place, part, two, other)
    keep, send = halves(keep + other, chip)
    other = swap(send, "dp", 4, 2)
    part = train(3, place)
    three = shift(part, "tensor", 4, 3)
    own = after(train(0, after(place, part, one)), other) + two + one + three

    near, far, across = swap(own, "tensor", 4, 1), swap(own, "tensor", 4, 2), swap(own, "dp", 4, 2)
    near = after(near, across)
    near_across = swap(near, "dp", 4, 2)
    asked = after(keep + other, near)
    asked = jnp.concatenate([asked] + [swap(asked, "tensor", 4, bit) for bit in (1, 2, 3)], axis=1)
    far = after(far, near_across)
    last = swap(after(own, far), "tensor", 4, 3)
    far = [far, swap(far, "dp", 4, 2)]
    asked = after(asked, far[0])
    blocks = in_order(asked, swap(asked, "dp", 4, 2), chip)
    total = gram(after(both_cores([own, across]), far[0]), None)
    last, far, blocks = after([last, far, blocks], total)
    last_across = swap(last, "dp", 4, 2)
    total = gram(after(both_cores([near, near_across]), last), total)
    last_across = after(last_across, total)
    blocks = in_order(blocks, swap(blocks, "dp", 4, 1), core)
    return own, both_cores(far) + both_cores([last, last_across]), total, blocks, me ^ jnp.arange(4, dtype=jnp.int32)


def anywhere(train, query, place, dp, tensor):
    asked = jnp.swapaxes(lax.all_gather(lax.psum(query(place), "dp"), "tensor"), 0, 1)
    asked = asked.reshape(asked.shape[0], -1)
    own = train(0, place)
    for by in range(1, tensor):
        own = own + shift(train(by, place), "tensor", tensor, by)
    every = lane_groups(lax.all_gather(own, ("dp", "tensor")))
    every = [every[i] for i in range(every.shape[0])]
    total = None
    for at in range(0, len(every) - 8, 8):
        total = gram(every[at : at + 8], total)
    return own, every[-8:], total, asked, jnp.arange(asked.shape[1] // LANES, dtype=jnp.int32)


def local(dp, tensor, acts, out_grads, proj_in, proj_out, query_acts, query_grads):
    me = lax.axis_index("tensor")
    place = [jnp.zeros_like(me), lax.axis_index("dp")]
    for by in range(tensor):
        place += [lax.rem(me + by, tensor), me]
    place = jnp.stack(place).astype(jnp.int32)
    tokens = acts.shape[0] // tensor

    def train(by, place):
        return project(acts, out_grads, proj_in, proj_out, SEQ, tokens, 512, place, 2 + 2 * by, 1)[0]

    def query(place):
        return project(query_acts, query_grads, proj_in, proj_out, QLEN, query_acts.shape[0], 256, place, 0, 1)[0]

    if dp == 4 and tensor == 4 and tokens == SEQ * LANES:
        own, toks, total, asked, order = square(train, query, place)
    else:
        own, toks, total, asked, order = anywhere(train, query, place, dp, tensor)
    examples = own.shape[1]
    padded = jnp.pad(own, ((0, 0), (0, LANES - examples)))
    return solve(toks, total, padded, asked, order)[:examples]


def solution(mesh):
    in_specs = (
        P(("groups", "dp"), "tensor"),
        P(("groups", "dp"), "tensor"),
        P(),
        P(),
        P(("groups", "tensor"), "dp"),
        P(("groups", "tensor"), "dp"),
    )
    out_specs = P(("groups", "dp", "tensor"), None)
    body = functools.partial(local, mesh.shape["dp"], mesh.shape["tensor"])
    return jax.shard_map(body, mesh=mesh, in_specs=in_specs, out_specs=out_specs, check_vma=False)
```
